32 devices in a mesh: tgt: 4 (over y, core), src: 8 (over z, x).
Axes of the slice: x: 2, y: 2, z: 4, core: 2. Of those that a mesh axis runs over, the one named last changes fastest.
Arguments:
- targets: bfloat16 [16, 64, 4096], P('tgt', 'src'), may hold values from -6 to 6
- sources: bfloat16 [8, 64, 4096], P('src', 'tgt'), may hold values from -6 to 6
- exponents: float32 [8], replicated, may hold values from 0.005 to 0.76
- coefficients: float32 [8], replicated, may hold values from -0.08 to 0.08
Outputs:
- exchange: float32 [64, 16, 4096], P('src', 'tgt')
The draws below stay inside these ranges and needn't reach their ends.
All inputs are finite; a program needn't handle non-finite values.
Results may differ from the reference program's by a relative error of at most 0.0063.
The reference program's roundings to bfloat16 on the way count: a program that leaves them out, or rounds other values in their place, can miss the bound.
Values may be sent and summed in bfloat16 or wider, within the bound.
A program may use at most 64 MiB of HBM per device.

```python
import math
import jax
import jax.numpy as jnp
from jax import lax

G = 64
GAUSS = 8
NT = 16
NS = 8


def gauss_terms(key):
    base_key = jax.random.fold_in(key, 7301)
    jitter_key, weight_key, sign_key = jax.random.split(base_key, 3)
    offsets = jax.random.uniform(jitter_key, (GAUSS,), jnp.float32, 0.4, 0.6)
    levels = (jnp.arange(GAUSS, dtype=jnp.float32) + offsets) / GAUSS
    exponents = 0.004 * jnp.exp(levels * math.log(250.0))
    weights = jax.random.uniform(weight_key, (GAUSS,), jnp.float32, 0.6, 1.4)
    ordering = jax.random.permutation(sign_key, GAUSS)
    sign_flip = jnp.where(ordering < 3, -1.0, 1.0).astype(jnp.float32)
    coefficients = 0.08 * sign_flip * weights * jnp.power(2.0 * exponents / math.pi, 0.75)
    return (exponents.astype(jnp.float32), coefficients.astype(jnp.float32))


def draw_exponents(key, part):
    return gauss_terms(key)[0]


def draw_coefficients(key, part):
    return gauss_terms(key)[1]


def raised(drawn, key, source, target, blocks, factor):
    owner, partner = [(jnp.arange(drawn.shape[axis_at]) // (drawn.shape[axis_at] // blocks)).reshape([-1 if axis == axis_at else 1 for axis in range(drawn.ndim)]) for axis_at in (source, target)]
    chosen = jax.random.permutation(key, blocks)[partner]
    strong = (owner == chosen) | (owner == (partner + blocks // 2) % blocks)
    return jnp.where(strong, factor * drawn, drawn)


def shard_levels(rng, shape, pieces, least, largest):
    factor_of = 1.0
    for dim, shards_of in pieces:
        draws = jax.random.uniform(jax.random.fold_in(jax.random.fold_in(rng, 6), dim), (shards_of,), jnp.float32, least / len(pieces), largest / len(pieces))
        factor_of = factor_of * jnp.repeat(jnp.exp(draws), shape[dim] // shards_of).reshape((-1,) + (1,) * (len(shape) - 1 - dim))
    return factor_of


def bell_draw(stream_key, dims, width, reach, shards=(), held_as=jnp.bfloat16):
    factor_of = shard_levels(stream_key, dims, shards, -0.22, 0.18) if shards else 1.0
    entries = jax.random.normal(stream_key, dims, jnp.float32) * width * factor_of
    return jnp.minimum(jnp.maximum(entries, -reach), reach).astype(held_as)


def noise_with(stream_key, dims, scale, limit, cuts, heavy, held_as=jnp.bfloat16):
    values = scale * jax.random.normal(stream_key, dims, jnp.float32)
    if cuts:
        values = values * shard_levels(stream_key, dims, cuts, -0.22, 0.18)
    return jnp.clip(raised(values, jax.random.fold_in(stream_key, 3), *heavy), -limit, limit).astype(held_as)


def setup_inputs(seed: int = 0) -> dict:
    key_of = jax.random.split(jax.random.key(seed), 5)
    targets = bell_draw(key_of[0], (NT, G, G * G), 1.0, 6.0, ((0, 4), (1, 8)))
    sources = noise_with(key_of[1], (NS, G, G * G), 1.0, 6.0, ((0, 8), (1, 4)), (0, 1, 8, 2.0))
    exponents = draw_exponents(jax.random.fold_in(key_of[4], 71), 0)
    coefficients = draw_coefficients(jax.random.fold_in(key_of[4], 71), 0)
    return dict(targets=targets, sources=sources, exponents=exponents, coefficients=coefficients)


def kernels(exponents, coefficients):
    grid_pos = jnp.arange(G, dtype=jnp.int32)
    distance = jnp.abs(grid_pos[:, None] - grid_pos[None, :])
    distance = jnp.minimum(distance, G - distance).astype(jnp.float32)
    gauss_table = jnp.exp(-exponents[:, None, None] * (distance * distance)[None])
    weighted = coefficients[:, None, None] * gauss_table
    return gauss_table.astype(jnp.bfloat16), weighted.astype(jnp.bfloat16)


def pair_term(target, source, kernel_table, weighted):
    density = (target.astype(jnp.float32) * source.astype(jnp.float32)).astype(jnp.bfloat16)
    density = lax.optimization_barrier(density).astype(jnp.float32)
    first_pass = jnp.einsum('gax,xm->gam', kernel_table.astype(jnp.float32), density).astype(jnp.bfloat16)
    first_pass = lax.optimization_barrier(first_pass).astype(jnp.float32).reshape(GAUSS, G, G, G)
    second_pass = jnp.einsum('gby,gayz->gabz', kernel_table.astype(jnp.float32), first_pass).astype(jnp.bfloat16)
    second_pass = lax.optimization_barrier(second_pass).astype(jnp.float32)
    potential = jnp.einsum('gcz,gabz->abc', weighted.astype(jnp.float32), second_pass).reshape(G, G * G)
    return potential * source.astype(jnp.float32)


def reference(targets, sources, exponents, coefficients):
    kernel_table, weighted = kernels(exponents, coefficients)

    def one_target(target):
        def add_source(summed, source):
            return summed + pair_term(target, source, kernel_table, weighted), None

        summed, _ = lax.scan(add_source, jnp.zeros((G, G * G), jnp.float32), sources)
        return -summed

    result = lax.map(one_target, targets)
    return jnp.transpose(result, (1, 0, 2))
```

```python
import functools
import math

import jax
import jax.numpy as jnp
import numpy as np
import ml_dtypes
from jax import lax
from jax.experimental import pallas as pl
from jax.experimental.pallas import tpu as pltpu
from jax.sharding import PartitionSpec as P

MESH = pl.DeviceIdType.MESH
BF16 = jnp.bfloat16
F32 = jnp.float32
YS = 8


def rounded(values):
    return values.astype(ml_dtypes.bfloat16).astype(np.float64)


@functools.lru_cache(None)
def basis(n):
    pos = np.arange(n, dtype=np.float64)
    columns, norms, freqs = [], [], []
    scales = 2.0 ** (np.arange(64) / 64)
    for k in range(n // 2 + 1):
        single = k == 0 or 2 * k == n
        best = None
        for phase in [0.0] if single else np.arange(32) * (2 * np.pi / n / 32):
            angle = 2 * np.pi * k * pos / n + phase
            pair = [np.cos(angle)] if single else [np.cos(angle), np.sin(angle)]
            for scale in scales:
                scaled = [scale * p for p in pair]
                err = sum(np.sum((rounded(p) - p) ** 2) for p in scaled) / scale**2
                if best is None or err < best[0] - 1e-15:
                    best = (err, scaled, scale)
        for p in best[1]:
            columns.append(p)
            norms.append(best[2] ** 2 * (n if single else n / 2))
            freqs.append(k)
    table = np.stack(columns, 1)
    cosines = np.cos(2 * np.pi * np.outer(np.array(freqs), pos) / n) / np.array(norms)[:, None]
    return table, cosines


def kernel(
    dims,
    tgt_ref, src_ref, exp_ref, coef_ref, cos_ref, wz_ref, wzt_ref, bx_ref, bxt_ref, by_ref, byt_ref,
    out_ref,
    sfull, tfull, s32, t32, work, spec, obuf, orecv, lam_ref, wl_ref,
    a_send, a_recv, b1_send, b1_recv, b2_send, b2_recv, b3_send, b3_recv, c_send, c_recv, local_sem,
):
    tn, sn, ni, xn, un, px, pb, m, n, nj = dims
    t = lax.axis_index("tgt")
    s = lax.axis_index("src")
    z, x = s // xn, s % xn
    u, c = t // 2, t % 2
    cn = 1 - c

    def at(tt, ss):
        return {"tgt": tt, "src": ss}

    barrier = pltpu.get_barrier_semaphore()
    for d in range(1, sn):
        pl.semaphore_signal(barrier, inc=1, device_id=at(t, (s + d) % sn), device_id_type=MESH)
    for e in range(1, un):
        pl.semaphore_signal(barrier, inc=1, device_id=at(((u + e) % un) * 2 + c, s), device_id_type=MESH)
    pl.semaphore_signal(barrier, inc=1, device_id=at(u * 2 + cn, s), device_id_type=MESH)
    pl.semaphore_wait(barrier, sn - 1 + un - 1 + 1)

    def remote(src, dst, send, recv, dev):
        return pltpu.make_async_remote_copy(
            src_ref=src, dst_ref=dst, send_sem=send, recv_sem=recv, device_id=dev, device_id_type=MESH
        )

    own_src = src_ref.at[0]
    sends = []

    def go(copy):
        copy.start()
        sends.append(copy)

    for d in range(1, ni):
        go(remote(own_src, sfull.at[z, t], b1_send.at[d], b1_recv.at[d], at(t, ((z + d) % ni) * xn + x)))
    own_copy = pltpu.make_async_copy(own_src, sfull.at[z, t], local_sem.at[0])
    own_copy.start()
    for d in range(1, sn):
        to = (s + d) % sn
        go(remote(tgt_ref.at[to // xn], tfull.at[s], a_send.at[d], a_recv.at[d], at(t, to)))
    tgt_copy = pltpu.make_async_copy(tgt_ref.at[z], tfull.at[s], local_sem.at[1])
    tgt_copy.start()

    def forward(d, block):
        src_z = (z + ni - d) % ni
        for e in range(1, un):
            go(remote(block, sfull.at[src_z, t], b2_send.at[d, e], b2_recv.at[d, e], at(((u + e) % un) * 2 + c, s)))
        go(remote(block, sfull.at[src_z, t], b3_send.at[d, 0], b3_recv.at[d, 0], at(u * 2 + cn, s)))

    forward(0, own_src)

    dist = lax.broadcasted_iota(jnp.int32, (exp_ref.shape[0], n), 1)
    dist = jnp.minimum(dist, n - dist).astype(F32)
    gauss = jnp.exp(-exp_ref[...] * (dist * dist))
    wgauss = (coef_ref[...] * gauss).astype(BF16).astype(F32)
    gauss = gauss.astype(BF16).astype(F32)
    dot = functools.partial(lax.dot_general, preferred_element_type=F32)
    hot = functools.partial(dot, precision=lax.Precision.HIGHEST)
    last = (((1,), (1,)), ((), ()))
    plain = (((1,), (0,)), ((), ()))
    lam_t = hot(cos_ref[...], gauss, last)
    lam = hot(gauss, cos_ref[...], last)
    lam_ref[...] = lam_t
    wl_ref[...] = hot(cos_ref[...], wgauss, last)
    lam_x = jnp.concatenate([lam] * nj, axis=1)
    lanes = nj * n

    def spectrum(q, carry):
        rows = wl_ref[pl.ds(pl.multiple_of(q * 8, 8), 8), :]
        left = (rows[:, None, :] * lam_ref[...][None]).reshape(8 * n, rows.shape[1])
        spec[pl.ds(pl.multiple_of(q * 8 * n, 8 * n), 8 * n), :] = hot(left, lam_x, plain)
        return carry

    lax.fori_loop(0, n // 8, spectrum, 0)

    for d in range(1, ni):
        src_z = (z + ni - d) % ni
        slot = sfull.at[src_z, t]
        remote(slot, slot, b1_send.at[d], b1_recv.at[d], at(t, s)).wait_recv()
        forward(d, slot)
    for d in range(ni):
        src_z = (z + ni - d) % ni
        for e in range(1, un):
            slot = sfull.at[src_z, ((u + un - e) % un) * 2 + c]
            remote(slot, slot, b2_send.at[d, e], b2_recv.at[d, e], at(t, s)).wait_recv()
            go(remote(slot, slot, b3_send.at[d, e], b3_recv.at[d, e], at(u * 2 + cn, s)))
    tgt_copy.wait()
    for d in range(1, sn):
        slot = tfull.at[(s + sn - d) % sn]
        remote(slot, slot, a_send.at[d], a_recv.at[d], at(t, s)).wait_recv()
    for k in range(sn):
        t32[k * px:(k + 1) * px, :] = tfull[k].astype(F32)
    own_copy.wait()
    for d in range(ni):
        src_z = (z + ni - d) % ni
        for e in range(un):
            slot = sfull.at[src_z, ((u + un - e) % un) * 2 + cn]
            remote(slot, slot, b3_send.at[d, e], b3_recv.at[d, e], at(t, s)).wait_recv()
    for j in range(nj):
        for k in range(tn):
            s32[j * n + k * pb:j * n + (k + 1) * pb, :] = sfull[j, k].astype(F32)

    width = YS * n

    def into_modes(k, carry):
        cols = pl.ds(pl.multiple_of(k * width, width), width)
        tile = t32[:, cols]
        dens = (s32[:, cols] * jnp.concatenate([tile] * nj, axis=0)).astype(BF16)
        first = dot(wz_ref[...], dens, last).astype(BF16)
        second = dot(first, bx_ref[...], plain)
        work[:, pl.ds(pl.multiple_of(k * YS, YS), YS), :] = second.reshape(n, YS, lanes)
        return carry

    lax.fori_loop(0, m // width, into_modes, 0)

    def in_modes(q, carry):
        group = pl.ds(q * nj, nj)
        rows = work[group].reshape(nj * n, lanes).astype(BF16)
        modes = dot(byt_ref[...], rows, plain)
        modes = (modes * spec[pl.ds(pl.multiple_of(q * nj * n, nj * n), nj * n), :]).astype(BF16)
        back = dot(by_ref[...], modes, plain).astype(BF16)
        back = dot(back, bxt_ref[...], plain)
        work[group] = back.reshape(nj, n, lanes)
        return carry

    lax.fori_loop(0, n // nj, in_modes, 0)

    def from_modes(k, carry):
        cols = pl.ds(pl.multiple_of(k * width, width), width)
        rows = work[:, pl.ds(pl.multiple_of(k * YS, YS), YS), :].reshape(YS * n, lanes).astype(BF16)
        pot = dot(rows, wzt_ref[...], (((0,), (0,)), ((), ())))
        prod = pot * s32[:, cols]
        total = prod[:n]
        for j in range(1, nj):
            total = total + prod[j * n:(j + 1) * n]
        total = -total
        for b in range(sn):
            obuf[b, :, cols] = total[b * px:(b + 1) * px].astype(BF16)
        return carry

    lax.fori_loop(0, m // width, from_modes, 0)

    for d in range(1, sn):
        to = (s + d) % sn
        go(remote(obuf.at[to], orecv.at[s], c_send.at[d], c_recv.at[d], at(t, to)))
    out_copy = pltpu.make_async_copy(obuf.at[s], orecv.at[s], local_sem.at[2])
    out_copy.start()
    out_copy.wait()
    for d in range(1, sn):
        slot = orecv.at[(s + sn - d) % sn]
        remote(slot, slot, c_send.at[d], c_recv.at[d], at(t, s)).wait_recv()
    for i in range(ni):
        total = orecv[i * xn].astype(F32)
        for k in range(1, xn):
            total = total + orecv[i * xn + k].astype(F32)
        out_ref[:, i, :] = total
    for copy in sends:
        copy.wait_send()


def shards(mesh_shape, targets, sources, exponents, coefficients):
    tn, sn = mesh_shape
    ni, px, m = targets.shape
    js, pb, _ = sources.shape
    n = px * sn
    xn = sn // ni
    un = tn // 2
    nj = ni * js
    assert js == 1 and m == n * n and sn % ni == 0 and tn % 2 == 0
    table, cosines = basis(n)
    eye = np.eye(YS)
    wz = np.einsum("zk,rs->krsz", table, eye).reshape(n * YS, YS * n)
    diag = np.kron(np.eye(nj), table)
    consts = [jnp.asarray(cosines, F32)] + [
        jnp.asarray(v.astype(ml_dtypes.bfloat16)) for v in (wz, wz, diag, diag.T, diag, diag.T)
    ]
    dims = (tn, sn, ni, xn, un, px, pb, m, n, nj)
    vmem = pl.BlockSpec(memory_space=pltpu.VMEM)
    gauss_count = exponents.shape[0]
    dma = pltpu.SemaphoreType.DMA
    return pl.pallas_call(
        functools.partial(kernel, dims),
        out_shape=jax.ShapeDtypeStruct((px, ni, m), F32),
        in_specs=[vmem] * 11,
        out_specs=vmem,
        scratch_shapes=[
            pltpu.VMEM((nj, tn, pb, m), BF16),
            pltpu.VMEM((sn, px, m), BF16),
            pltpu.VMEM((nj * n, m), F32),
            pltpu.VMEM((n, m), F32),
            pltpu.VMEM((n, n, nj * n), F32),
            pltpu.VMEM((n * n, nj * n), F32),
            pltpu.VMEM((sn, px, m), BF16),
            pltpu.VMEM((sn, px, m), BF16),
            pltpu.VMEM((n, gauss_count), F32),
            pltpu.VMEM((n, gauss_count), F32),
            dma((sn,)), dma((sn,)),
            dma((ni,)), dma((ni,)),
            dma((ni, un)), dma((ni, un)),
            dma((ni, un)), dma((ni, un)),
            dma((sn,)), dma((sn,)),
            dma((3,)),
        ],
        compiler_params=pltpu.CompilerParams(
            collective_id=0, has_side_effects=True, vmem_limit_bytes=48 * 1024 * 1024
        ),
    )(targets, sources, exponents[:, None], coefficients[:, None], *consts)


def solution(mesh):
    placed = (P("tgt", "src", None), P("src", "tgt", None), P(), P())
    mesh_shape = (mesh.shape["tgt"], mesh.shape["src"])
    return jax.shard_map(
        functools.partial(shards, mesh_shape),
        mesh=mesh, in_specs=placed, out_specs=P("src", "tgt", None), check_vma=False,
    )
```

```python
import functools
import math

import jax
import jax.numpy as jnp
import numpy as np
import ml_dtypes
from jax import lax
from jax.experimental import pallas as pl
from jax.experimental.pallas import tpu as pltpu
from jax.sharding import PartitionSpec as P

MESH = pl.DeviceIdType.MESH
BF16 = jnp.bfloat16
F32 = jnp.float32
YS = 8
PARTS = 2
CHUNKS = 4


def rounded(values):
    return values.astype(ml_dtypes.bfloat16).astype(np.float64)


@functools.lru_cache(None)
def basis(n):
    pos = np.arange(n, dtype=np.float64)
    columns, norms, freqs = [], [], []
    scales = 2.0 ** (np.arange(64) / 64)
    for k in range(n // 2 + 1):
        single = k == 0 or 2 * k == n
        best = None
        for phase in [0.0] if single else np.arange(32) * (2 * np.pi / n / 32):
            angle = 2 * np.pi * k * pos / n + phase
            pair = [np.cos(angle)] if single else [np.cos(angle), np.sin(angle)]
            for scale in scales:
                scaled = [scale * p for p in pair]
                err = sum(np.sum((rounded(p) - p) ** 2) for p in scaled) / scale**2
                if best is None or err < best[0] - 1e-15:
                    best = (err, scaled, scale)
        for p in best[1]:
            columns.append(p)
            norms.append(best[2] ** 2 * (n if single else n / 2))
            freqs.append(k)
    table = np.stack(columns, 1)
    cosines = np.cos(2 * np.pi * np.outer(np.array(freqs), pos) / n) / np.array(norms)[:, None]
    return table, cosines


def kernel(
    dims,
    tgt_ref, src_ref, exp_ref, coef_ref, cos_hbm, wz_hbm, diag_hbm, diagt_hbm,
    out_ref,
    cos_ref, wz_ref, diag_ref, diagt_ref,
    sfull, tfull, s32, t32, work, spec, acc, obuf, xrecv, zbuf, zrecv, lam_ref, wl_ref,
    a1_send, a1_recv, a2_send, a2_recv, b1_send, b1_recv, b2_send, b2_recv, b3_send, b3_recv,
    x_send, x_recv, z_send, z_recv, own_sem, const_sem,
):
    tn, sn, ni, xn, un, px, pb, m, n, nj = dims
    t = lax.axis_index("tgt")
    s = lax.axis_index("src")
    z, x = s // xn, s % xn
    u, c = t // 2, t % 2
    partner = {"tgt": u * 2 + 1 - c, "src": s}

    def z_peer(d):
        return {"tgt": t, "src": ((z + d) % ni) * xn + x}

    def x_peer(f):
        return {"tgt": t, "src": z * xn + (x + f) % xn}

    def u_peer(e):
        return {"tgt": ((u + e) % un) * 2 + c, "src": s}

    consts = [
        pltpu.make_async_copy(a, b, const_sem.at[k])
        for k, (a, b) in enumerate(
            [(cos_hbm, cos_ref), (wz_hbm, wz_ref), (diag_hbm, diag_ref), (diagt_hbm, diagt_ref)]
        )
    ]
    for copy in consts:
        copy.start()

    peers = [z_peer(d) for d in range(1, ni)] + [x_peer(f) for f in range(1, xn)]
    peers += [u_peer(e) for e in range(1, un)] + [partner]
    barrier = pltpu.get_barrier_semaphore()
    for peer in peers:
        pl.semaphore_signal(barrier, inc=1, device_id=peer, device_id_type=MESH)
    pl.semaphore_wait(barrier, len(peers))

    def remote(src, dst, send, recv, dev):
        return pltpu.make_async_remote_copy(
            src_ref=src, dst_ref=dst, send_sem=send, recv_sem=recv, device_id=dev, device_id_type=MESH
        )

    sends = []

    def go(copy):
        copy.start()
        sends.append(copy)

    def arrived(slot, send, recv):
        remote(slot, slot, send, recv, partner).wait_recv()

    part = m // PARTS

    def piece(h):
        return pl.ds(h * part, part)

    def from_z(d):
        return (z + ni - d) % ni

    def pass_source(h, d, block):
        slot = sfull.at[from_z(d), t, :, piece(h)]
        for e in range(1, un):
            go(remote(block, slot, b2_send.at[h, d, e], b2_recv.at[h, d, e], u_peer(e)))
        go(remote(block, slot, b3_send.at[h, d, 0], b3_recv.at[h, d, 0], partner))

    def pass_target(h, d, block):
        slot = tfull.at[from_z(d) * xn + x, :, piece(h)]
        for f in range(1, xn):
            go(remote(block, slot, a2_send.at[h, d, f], a2_recv.at[h, d, f], x_peer(f)))

    own = []
    for h in range(PARTS):
        src_own, tgt_own = src_ref.at[0, :, piece(h)], tgt_ref.at[z, :, piece(h)]
        for d in range(1, ni):
            go(remote(src_own, sfull.at[z, t, :, piece(h)], b1_send.at[h, d], b1_recv.at[h, d], z_peer(d)))
        for d in range(1, ni):
            go(remote(
                tgt_ref.at[(z + d) % ni, :, piece(h)], tfull.at[s, :, piece(h)],
                a1_send.at[h, d], a1_recv.at[h, d], z_peer(d),
            ))
        pass_source(h, 0, src_own)
        pass_target(h, 0, tgt_own)
        own.append(pltpu.make_async_copy(src_own, sfull.at[z, t, :, piece(h)], own_sem.at[h, 0]))
        own.append(pltpu.make_async_copy(tgt_own, tfull.at[s, :, piece(h)], own_sem.at[h, 1]))
    for copy in own:
        copy.start()

    dist = lax.broadcasted_iota(jnp.int32, (1, n), 1)
    dist = jnp.minimum(dist, n - dist).astype(F32)
    count = exp_ref.shape[0]
    gauss = jnp.concatenate([jnp.exp(-exp_ref[g] * (dist * dist)) for g in range(count)], axis=0)
    wgauss = jnp.concatenate([coef_ref[g] * gauss[g:g + 1] for g in range(count)], axis=0)
    wgauss = wgauss.astype(BF16).astype(F32)
    gauss = gauss.astype(BF16).astype(F32)
    dot = functools.partial(lax.dot_general, preferred_element_type=F32)
    hot = functools.partial(dot, precision=lax.Precision.HIGHEST)
    last = (((1,), (1,)), ((), ()))
    plain = (((1,), (0,)), ((), ()))
    for copy in consts:
        copy.wait()
    lam_ref[...] = hot(cos_ref[...], gauss, last)
    wl_ref[...] = hot(cos_ref[...], wgauss, last)
    lam = hot(gauss, cos_ref[...], last)
    lam_x = jnp.concatenate([lam] * nj, axis=1)
    lanes = nj * n
    steps = list(range(n // 8))

    def spectrum():
        if steps:
            q = steps.pop(0)
            rows = wl_ref[q * 8:(q + 1) * 8, :]
            left = (rows[:, None, :] * lam_ref[...][None]).reshape(8 * n, count)
            spec[q * 8 * n:(q + 1) * 8 * n, :] = hot(left, lam_x, plain)

    spectrum()
    for h in range(PARTS):
        for d in range(1, ni):
            slot = sfull.at[from_z(d), t, :, piece(h)]
            arrived(slot, b1_send.at[h, d], b1_recv.at[h, d])
            pass_source(h, d, slot)
            spectrum()
        for d in range(1, ni):
            slot = tfull.at[from_z(d) * xn + x, :, piece(h)]
            arrived(slot, a1_send.at[h, d], a1_recv.at[h, d])
            pass_target(h, d, slot)
    while steps:
        spectrum()
    for copy in own:
        copy.wait()

    width = YS * n

    def into_modes(k, carry):
        cols = pl.ds(pl.multiple_of(k * width, width), width)
        tile = t32[:, cols]
        dens = (s32[:, cols] * jnp.concatenate([tile] * nj, axis=0)).astype(BF16)
        first = dot(wz_ref[...], dens, last).astype(BF16)
        second = dot(first, diag_ref[...], plain)
        work[:, pl.ds(pl.multiple_of(k * YS, YS), YS), :] = second.reshape(n, YS, lanes)
        return carry

    def pass_to_partner(h):
        for d in range(ni):
            for e in range(1, un):
                slot = sfull.at[from_z(d), ((u + un - e) % un) * 2 + c, :, piece(h)]
                arrived(slot, b2_send.at[h, d, e], b2_recv.at[h, d, e])
                go(remote(slot, slot, b3_send.at[h, d, e], b3_recv.at[h, d, e], partner))

    for h in range(PARTS):
        pass_to_partner(h)
        for d in range(ni):
            for f in range(1, xn):
                slot = tfull.at[from_z(d) * xn + (x + xn - f) % xn, :, piece(h)]
                arrived(slot, a2_send.at[h, d, f], a2_recv.at[h, d, f])
        here = slice(h * part, (h + 1) * part)
        for k in range(sn):
            t32[k * px:(k + 1) * px, here] = tfull[k, :, here].astype(F32)
        for d in range(ni):
            for e in range(un):
                slot = sfull.at[from_z(d), ((u + un - e) % un) * 2 + 1 - c, :, piece(h)]
                arrived(slot, b3_send.at[h, d, e], b3_recv.at[h, d, e])
        for j in range(nj):
            for k in range(tn):
                s32[j * n + k * pb:j * n + (k + 1) * pb, here] = sfull[j, k, :, here].astype(F32)
        lax.fori_loop(h * part // width, (h + 1) * part // width, into_modes, 0, unroll=2)

    def in_modes(q, carry):
        group = pl.ds(q * nj, nj)
        rows = work[group].reshape(nj * n, lanes).astype(BF16)
        modes = dot(diagt_ref[...], rows, plain)
        modes = (modes * spec[pl.ds(pl.multiple_of(q * nj * n, nj * n), nj * n), :]).astype(BF16)
        back = dot(diag_ref[...], modes, plain).astype(BF16)
        back = dot(back, diagt_ref[...], plain)
        work[group] = back.reshape(nj, n, lanes)
        return carry

    lax.fori_loop(0, n // nj, in_modes, 0, unroll=4)

    def from_modes(k, carry):
        cols = pl.ds(pl.multiple_of(k * width, width), width)
        rows = work[:, pl.ds(pl.multiple_of(k * YS, YS), YS), :].reshape(YS * n, lanes).astype(BF16)
        pot = dot(rows, wz_ref[...], (((0,), (0,)), ((), ())))
        prod = pot * s32[:, cols]
        total = prod[:n]
        for j in range(1, nj):
            total = total + prod[j * n:(j + 1) * n]
        total = -total
        for b in range(sn):
            value = total[b * px:(b + 1) * px]
            acc[b % xn, b // xn, :, cols] = value
            obuf[b % xn, b // xn, :, cols] = value.astype(BF16)
        return carry

    chunk = m // CHUNKS

    def add_up(k):
        cols = pl.ds(k * chunk, chunk)
        for f in range(1, xn):
            arrived(xrecv.at[(x + xn - f) % xn, :, :, cols], x_send.at[k, f], x_recv.at[k, f])
        total = acc[x, :, :, cols]
        for f in range(1, xn):
            total = total + xrecv[(x + xn - f) % xn, :, :, cols].astype(F32)
        zbuf[:, :, cols] = total.astype(BF16)
        for d in range(1, ni):
            to = (z + d) % ni
            go(remote(zbuf.at[to, :, cols], zrecv.at[z, :, cols], z_send.at[k, d], z_recv.at[k, d], z_peer(d)))
        zrecv[z, :, cols] = zbuf[z, :, cols]

    for k in range(CHUNKS):
        cols = pl.ds(k * chunk, chunk)
        lax.fori_loop(k * chunk // width, (k + 1) * chunk // width, from_modes, 0, unroll=2)
        for f in range(1, xn):
            to = (x + f) % xn
            go(remote(
                obuf.at[to, :, :, cols], xrecv.at[x, :, :, cols], x_send.at[k, f], x_recv.at[k, f], x_peer(f)
            ))
        if k:
            add_up(k - 1)
    add_up(CHUNKS - 1)

    for k in range(CHUNKS):
        cols = pl.ds(k * chunk, chunk)
        for d in range(1, ni):
            arrived(zrecv.at[from_z(d), :, cols], z_send.at[k, d], z_recv.at[k, d])
        for i in range(ni):
            out_ref[:, i, cols] = zrecv[i, :, cols].astype(F32)
    for copy in sends:
        copy.wait_send()


def shards(mesh_shape, targets, sources, exponents, coefficients):
    tn, sn = mesh_shape
    ni, px, m = targets.shape
    js, pb, _ = sources.shape
    n = px * sn
    xn = sn // ni
    un = tn // 2
    nj = ni * js
    assert js == 1 and m == n * n and sn % ni == 0 and tn % 2 == 0
    table, cosines = basis(n)
    wz = np.einsum("zk,rs->krsz", table, np.eye(YS)).reshape(n * YS, YS * n)
    diag = np.kron(np.eye(nj), table)
    consts = [jnp.asarray(cosines, F32)] + [
        jnp.asarray(v.astype(ml_dtypes.bfloat16)) for v in (wz, diag, diag.T)
    ]
    dims = (tn, sn, ni, xn, un, px, pb, m, n, nj)
    anywhere = pl.BlockSpec(memory_space=pl.ANY)
    scalars = pl.BlockSpec(memory_space=pltpu.SMEM)
    gauss_count = exponents.shape[0]
    dma = pltpu.SemaphoreType.DMA

    def pair(*shape):
        return [dma(shape), dma(shape)]

    return pl.pallas_call(
        functools.partial(kernel, dims),
        out_shape=jax.ShapeDtypeStruct((px, ni, m), F32),
        in_specs=[anywhere, anywhere, scalars, scalars] + [anywhere] * 4,
        out_specs=pl.BlockSpec(memory_space=pltpu.VMEM),
        scratch_shapes=[
            pltpu.VMEM(consts[0].shape, F32),
            *[pltpu.VMEM(v.shape, BF16) for v in consts[1:]],
            pltpu.VMEM((nj, tn, pb, m), BF16),
            pltpu.VMEM((sn, px, m), BF16),
            pltpu.VMEM((nj * n, m), F32),
            pltpu.VMEM((n, m), F32),
            pltpu.VMEM((n, n, nj * n), F32),
            pltpu.VMEM((n * n, nj * n), F32),
            pltpu.VMEM((xn, ni, px, m), F32),
            pltpu.VMEM((xn, ni, px, m), BF16),
            pltpu.VMEM((xn, ni, px, m), BF16),
            pltpu.VMEM((ni, px, m), BF16),
            pltpu.VMEM((ni, px, m), BF16),
            pltpu.VMEM((n, gauss_count), F32),
            pltpu.VMEM((n, gauss_count), F32),
            *pair(PARTS, ni), *pair(PARTS, ni, xn),
            *pair(PARTS, ni), *pair(PARTS, ni, un), *pair(PARTS, ni, un),
            *pair(CHUNKS, xn), *pair(CHUNKS, ni),
            dma((PARTS, 2)), dma((4,)),
        ],
        compiler_params=pltpu.CompilerParams(
            collective_id=0, has_side_effects=True, vmem_limit_bytes=48 * 1024 * 1024
        ),
    )(targets, sources, exponents, coefficients, *consts)


def solution(mesh):
    placed = (P("tgt", "src", None), P("src", "tgt", None), P(), P())
    mesh_shape = (mesh.shape["tgt"], mesh.shape["src"])
    return jax.shard_map(
        functools.partial(shards, mesh_shape),
        mesh=mesh, in_specs=placed, out_specs=P("src", "tgt", None), check_vma=False,
    )
```

```python
import functools
import math

import jax
import jax.numpy as jnp
import numpy as np
import ml_dtypes
from jax import lax
from jax.experimental import pallas as pl
from jax.experimental.pallas import tpu as pltpu
from jax.sharding import PartitionSpec as P

MESH = pl.DeviceIdType.MESH
BF16 = jnp.bfloat16
F32 = jnp.float32
YS = 8
PARTS = 2
CHUNKS = 4


def rounded(values):
    return values.astype(ml_dtypes.bfloat16).astype(np.float64)


@functools.lru_cache(None)
def basis(n):
    pos = np.arange(n, dtype=np.float64)
    columns, norms, freqs = [], [], []
    scales = 2.0 ** (np.arange(64) / 64)
    for k in range(n // 2 + 1):
        single = k == 0 or 2 * k == n
        best = None
        for phase in [0.0] if single else np.arange(32) * (2 * np.pi / n / 32):
            angle = 2 * np.pi * k * pos / n + phase
            pair = [np.cos(angle)] if single else [np.cos(angle), np.sin(angle)]
            for scale in scales:
                scaled = [scale * p for p in pair]
                err = sum(np.sum((rounded(p) - p) ** 2) for p in scaled) / scale**2
                if best is None or err < best[0] - 1e-15:
                    best = (err, scaled, scale)
        for p in best[1]:
            columns.append(p)
            norms.append(best[2] ** 2 * (n if single else n / 2))
            freqs.append(k)
    table = np.stack(columns, 1)
    cosines = np.cos(2 * np.pi * np.outer(np.array(freqs), pos) / n) / np.array(norms)[:, None]
    return table, cosines


def kernel(
    dims,
    tgt_ref, src_ref, exp_ref, coef_ref, cos_hbm, wz_hbm, diag_hbm, diagt_hbm,
    out_ref,
    cos_ref, wz_ref, diag_ref, diagt_ref,
    sfull, tfull, s32, t32, work, spec, acc, obuf, xrecv, zbuf, zrecv, lam_ref, wl_ref,
    a1_send, a1_recv, a2_send, a2_recv, b1_send, b1_recv, b2_send, b2_recv, b3_send, b3_recv,
    x_send, x_recv, z_send, z_recv, own_sem, const_sem,
):
    tn, sn, ni, xn, un, px, pb, m, n, nj = dims
    t = lax.axis_index("tgt")
    s = lax.axis_index("src")
    z, x = s // xn, s % xn
    u, c = t // 2, t % 2
    partner = {"tgt": u * 2 + 1 - c, "src": s}

    def across(d):
        to = z
        for bit in [1 << k for k in range(ni.bit_length()) if d >> k & 1]:
            to = to + bit - 2 * bit * (z // bit % 2)
        return to

    def z_peer(d):
        return {"tgt": t, "src": across(d) * xn + x}

    def x_peer(f):
        return {"tgt": t, "src": z * xn + (x + f) % xn}

    def u_peer(e):
        return {"tgt": ((u + e) % un) * 2 + c, "src": s}

    consts = [
        pltpu.make_async_copy(a, b, const_sem.at[k])
        for k, (a, b) in enumerate(
            [(cos_hbm, cos_ref), (wz_hbm, wz_ref), (diag_hbm, diag_ref), (diagt_hbm, diagt_ref)]
        )
    ]
    for copy in consts:
        copy.start()

    peers = [z_peer(d) for d in range(1, ni)] + [x_peer(f) for f in range(1, xn)]
    peers += [u_peer(e) for e in range(1, un)] + [partner]
    barrier = pltpu.get_barrier_semaphore()
    for peer in peers:
        pl.semaphore_signal(barrier, inc=1, device_id=peer, device_id_type=MESH)
    pl.semaphore_wait(barrier, len(peers))

    def remote(src, dst, send, recv, dev):
        return pltpu.make_async_remote_copy(
            src_ref=src, dst_ref=dst, send_sem=send, recv_sem=recv, device_id=dev, device_id_type=MESH
        )

    sends = []

    def go(copy):
        copy.start()
        sends.append(copy)

    def arrived(slot, send, recv):
        remote(slot, slot, send, recv, partner).wait_recv()

    part = m // PARTS

    def piece(h):
        return pl.ds(h * part, part)

    def hand_on(h, d, bit, block):
        r = d ^ bit
        slot = sfull.at[across(d), t, :, piece(h)]
        go(remote(block, slot, b1_send.at[h, r], b1_recv.at[h, r], z_peer(bit)))

    def pass_source(h, d, block):
        slot = sfull.at[across(d), t, :, piece(h)]
        for e in range(1, un):
            go(remote(block, slot, b2_send.at[h, d, e], b2_recv.at[h, d, e], u_peer(e)))
        go(remote(block, slot, b3_send.at[h, d, 0], b3_recv.at[h, d, 0], partner))

    def pass_target(h, d, block):
        slot = tfull.at[across(d) * xn + x, :, piece(h)]
        for f in range(1, xn):
            go(remote(block, slot, a2_send.at[h, d, f], a2_recv.at[h, d, f], x_peer(f)))

    own = []
    for h in range(PARTS):
        src_own, tgt_own = src_ref.at[0, :, piece(h)], tgt_ref.at[z, :, piece(h)]
        for d in range(1, ni):
            if d & (d - 1) == 0:
                hand_on(h, 0, d, src_own)
        for d in range(1, ni):
            go(remote(
                tgt_ref.at[across(d), :, piece(h)], tfull.at[s, :, piece(h)],
                a1_send.at[h, d], a1_recv.at[h, d], z_peer(d),
            ))
        pass_source(h, 0, src_own)
        pass_target(h, 0, tgt_own)
        own.append(pltpu.make_async_copy(src_own, sfull.at[z, t, :, piece(h)], own_sem.at[h, 0]))
        own.append(pltpu.make_async_copy(tgt_own, tfull.at[s, :, piece(h)], own_sem.at[h, 1]))
    for copy in own:
        copy.start()

    dist = lax.broadcasted_iota(jnp.int32, (1, n), 1)
    dist = jnp.minimum(dist, n - dist).astype(F32)
    count = exp_ref.shape[0]
    gauss = jnp.concatenate([jnp.exp(-exp_ref[g] * (dist * dist)) for g in range(count)], axis=0)
    wgauss = jnp.concatenate([coef_ref[g] * gauss[g:g + 1] for g in range(count)], axis=0)
    wgauss = wgauss.astype(BF16).astype(F32)
    gauss = gauss.astype(BF16).astype(F32)
    dot = functools.partial(lax.dot_general, preferred_element_type=F32)
    hot = functools.partial(dot, precision=lax.Precision.HIGHEST)
    last = (((1,), (1,)), ((), ()))
    plain = (((1,), (0,)), ((), ()))
    for copy in consts:
        copy.wait()
    lam_ref[...] = hot(cos_ref[...], gauss, last)
    wl_ref[...] = hot(cos_ref[...], wgauss, last)
    lam = hot(gauss, cos_ref[...], last)
    lam_x = jnp.concatenate([lam] * nj, axis=1)
    lanes = nj * n
    steps = list(range(n // 8))

    def spectrum():
        if steps:
            q = steps.pop(0)
            rows = wl_ref[q * 8:(q + 1) * 8, :]
            left = (rows[:, None, :] * lam_ref[...][None]).reshape(8 * n, count)
            spec[q * 8 * n:(q + 1) * 8 * n, :] = hot(left, lam_x, plain)

    spectrum()
    for h in range(PARTS):
        for d in sorted(range(1, ni), key=lambda r: -(r & -r)):
            slot = sfull.at[across(d), t, :, piece(h)]
            arrived(slot, b1_send.at[h, d], b1_recv.at[h, d])
            for bit in [1 << k for k in range(ni.bit_length()) if 1 << k < (d & -d)]:
                hand_on(h, d, bit, slot)
            pass_source(h, d, slot)
            spectrum()
        for d in range(1, ni):
            slot = tfull.at[across(d) * xn + x, :, piece(h)]
            arrived(slot, a1_send.at[h, d], a1_recv.at[h, d])
            pass_target(h, d, slot)
    while steps:
        spectrum()
    for copy in own:
        copy.wait()

    width = YS * n

    def into_modes(k, carry):
        cols = pl.ds(pl.multiple_of(k * width, width), width)
        tile = t32[:, cols]
        dens = (s32[:, cols] * jnp.concatenate([tile] * nj, axis=0)).astype(BF16)
        first = dot(wz_ref[...], dens, last).astype(BF16)
        second = dot(first, diag_ref[...], plain)
        work[:, pl.ds(pl.multiple_of(k * YS, YS), YS), :] = second.reshape(n, YS, lanes)
        return carry

    def pass_to_partner(h):
        for d in range(ni):
            for e in range(1, un):
                slot = sfull.at[across(d), ((u + un - e) % un) * 2 + c, :, piece(h)]
                arrived(slot, b2_send.at[h, d, e], b2_recv.at[h, d, e])
                go(remote(slot, slot, b3_send.at[h, d, e], b3_recv.at[h, d, e], partner))

    for h in range(PARTS):
        pass_to_partner(h)
        for d in range(ni):
            for f in range(1, xn):
                slot = tfull.at[across(d) * xn + (x + xn - f) % xn, :, piece(h)]
                arrived(slot, a2_send.at[h, d, f], a2_recv.at[h, d, f])
        here = slice(h * part, (h + 1) * part)
        for k in range(sn):
            t32[k * px:(k + 1) * px, here] = tfull[k, :, here].astype(F32)
        for d in range(ni):
            for e in range(un):
                slot = sfull.at[across(d), ((u + un - e) % un) * 2 + 1 - c, :, piece(h)]
                arrived(slot, b3_send.at[h, d, e], b3_recv.at[h, d, e])
        for j in range(nj):
            for k in range(tn):
                s32[j * n + k * pb:j * n + (k + 1) * pb, here] = sfull[j, k, :, here].astype(F32)
        lax.fori_loop(h * part // width, (h + 1) * part // width, into_modes, 0, unroll=2)

    def in_modes(q, carry):
        group = pl.ds(q * nj, nj)
        rows = work[group].reshape(nj * n, lanes).astype(BF16)
        modes = dot(diagt_ref[...], rows, plain)
        modes = (modes * spec[pl.ds(pl.multiple_of(q * nj * n, nj * n), nj * n), :]).astype(BF16)
        back = dot(diag_ref[...], modes, plain).astype(BF16)
        back = dot(back, diagt_ref[...], plain)
        work[group] = back.reshape(nj, n, lanes)
        return carry

    lax.fori_loop(0, n // nj, in_modes, 0, unroll=4)

    def from_modes(k, carry):
        cols = pl.ds(pl.multiple_of(k * width, width), width)
        rows = work[:, pl.ds(pl.multiple_of(k * YS, YS), YS), :].reshape(YS * n, lanes).astype(BF16)
        pot = dot(rows, wz_ref[...], (((0,), (0,)), ((), ())))
        prod = pot * s32[:, cols]
        total = prod[:n]
        for j in range(1, nj):
            total = total + prod[j * n:(j + 1) * n]
        total = -total
        for b in range(sn):
            value = total[b * px:(b + 1) * px]
            acc[b % xn, b // xn, :, cols] = value
            obuf[b % xn, b // xn, :, cols] = value.astype(BF16)
        return carry

    chunk = m // CHUNKS

    def add_up(k):
        cols = pl.ds(k * chunk, chunk)
        for f in range(1, xn):
            arrived(xrecv.at[(x + xn - f) % xn, :, :, cols], x_send.at[k, f], x_recv.at[k, f])
        total = acc[x, :, :, cols]
        for f in range(1, xn):
            total = total + xrecv[(x + xn - f) % xn, :, :, cols].astype(F32)
        zbuf[:, :, cols] = total.astype(BF16)
        for d in range(1, ni):
            to = across(d)
            go(remote(zbuf.at[to, :, cols], zrecv.at[z, :, cols], z_send.at[k, d], z_recv.at[k, d], z_peer(d)))
        zrecv[z, :, cols] = zbuf[z, :, cols]

    for k in range(CHUNKS):
        cols = pl.ds(k * chunk, chunk)
        lax.fori_loop(k * chunk // width, (k + 1) * chunk // width, from_modes, 0, unroll=2)
        for f in range(1, xn):
            to = (x + f) % xn
            go(remote(
                obuf.at[to, :, :, cols], xrecv.at[x, :, :, cols], x_send.at[k, f], x_recv.at[k, f], x_peer(f)
            ))
        if k:
            add_up(k - 1)
    add_up(CHUNKS - 1)

    for k in range(CHUNKS):
        cols = pl.ds(k * chunk, chunk)
        for d in range(1, ni):
            arrived(zrecv.at[across(d), :, cols], z_send.at[k, d], z_recv.at[k, d])
        for i in range(ni):
            out_ref[:, i, cols] = zrecv[i, :, cols].astype(F32)
    for copy in sends:
        copy.wait_send()


def shards(mesh_shape, targets, sources, exponents, coefficients):
    tn, sn = mesh_shape
    ni, px, m = targets.shape
    js, pb, _ = sources.shape
    n = px * sn
    xn = sn // ni
    un = tn // 2
    nj = ni * js
    assert js == 1 and m == n * n and sn % ni == 0 and ni & (ni - 1) == 0 and tn % 2 == 0
    table, cosines = basis(n)
    wz = np.einsum("zk,rs->krsz", table, np.eye(YS)).reshape(n * YS, YS * n)
    diag = np.kron(np.eye(nj), table)
    consts = [jnp.asarray(cosines, F32)] + [
        jnp.asarray(v.astype(ml_dtypes.bfloat16)) for v in (wz, diag, diag.T)
    ]
    dims = (tn, sn, ni, xn, un, px, pb, m, n, nj)
    anywhere = pl.BlockSpec(memory_space=pltpu.HBM)
    scalars = pl.BlockSpec(memory_space=pltpu.SMEM)
    gauss_count = exponents.shape[0]
    dma = pltpu.SemaphoreType.DMA

    def pair(*shape):
        return [dma(shape), dma(shape)]

    return pl.pallas_call(
        functools.partial(kernel, dims),
        out_shape=jax.ShapeDtypeStruct((px, ni, m), F32),
        in_specs=[anywhere, anywhere, scalars, scalars] + [anywhere] * 4,
        out_specs=pl.BlockSpec(memory_space=pltpu.VMEM),
        scratch_shapes=[
            pltpu.VMEM(consts[0].shape, F32),
            *[pltpu.VMEM(v.shape, BF16) for v in consts[1:]],
            pltpu.VMEM((nj, tn, pb, m), BF16),
            pltpu.VMEM((sn, px, m), BF16),
            pltpu.VMEM((nj * n, m), F32),
            pltpu.VMEM((n, m), F32),
            pltpu.VMEM((n, n, nj * n), F32),
            pltpu.VMEM((n * n, nj * n), F32),
            pltpu.VMEM((xn, ni, px, m), F32),
            pltpu.VMEM((xn, ni, px, m), BF16),
            pltpu.VMEM((xn, ni, px, m), BF16),
            pltpu.VMEM((ni, px, m), BF16),
            pltpu.VMEM((ni, px, m), BF16),
            pltpu.VMEM((n, gauss_count), F32),
            pltpu.VMEM((n, gauss_count), F32),
            *pair(PARTS, ni), *pair(PARTS, ni, xn),
            *pair(PARTS, ni), *pair(PARTS, ni, un), *pair(PARTS, ni, un),
            *pair(CHUNKS, xn), *pair(CHUNKS, ni),
            dma((PARTS, 2)), dma((4,)),
        ],
        compiler_params=pltpu.CompilerParams(
            collective_id=0, has_side_effects=True, vmem_limit_bytes=62 * 1024 * 1024
        ),
    )(targets, sources, exponents, coefficients, *consts)


def solution(mesh):
    placed = (P("tgt", "src", None), P("src", "tgt", None), P(), P())
    mesh_shape = (mesh.shape["tgt"], mesh.shape["src"])
    return jax.shard_map(
        functools.partial(shards, mesh_shape),
        mesh=mesh, in_specs=placed, out_specs=P("src", "tgt", None), check_vma=False,
    )
```
